32 devices in a mesh: tm: 16 (over z, y, x), traj: 2 (over core).
Axes of the slice: x: 2, y: 2, z: 4, core: 2. Of those that a mesh axis runs over, the one named last changes fastest.
Arguments:
- init_state: float32 [32, 256], P('traj'), may hold values from -6 to 6
- nominal: bfloat16 [1024, 32, 256], P('tm', 'traj'), may hold values from -6 to 6
- target: bfloat16 [1024, 32, 256], P('tm', 'traj'), may hold values from -6 to 6
- decay: float32 [1024, 256], P('tm'), may hold values from 0.4 to 1, as said below
- gain_k: bfloat16 [1024, 64, 256], P('tm'), may hold values from -0.01171875 to 0.01171875
- ctrl_b: bfloat16 [256, 64], replicated, may hold values from -0.75 to 0.75
- w_in: bfloat16 [256, 2048], replicated, may hold values from -0.375 to 0.375
- hidden_bias: float32 [2048], replicated, may hold values from -4 to 4
- w_out: bfloat16 [2048, 256], replicated, may hold values from -0.125 to 0.125
Outputs:
- states: float32 [1024, 32, 256], P('tm', 'traj')
- grad_in: float32 [256, 2048], P(None, 'traj')
- output_weight_gradient: float32 [2048, 256], P('traj')
- grad_bias: float32 [2048], P('traj')
The draws below stay inside these ranges and needn't reach their ends.
Inputs may be any that keep to these rules, and one draw needn't show every extreme that they name: Every entry of decay is below 1.
All inputs are finite; a program needn't handle non-finite values.
Results may differ from the reference program's by a relative error of at most 0.0015.
Values sent between devices are 32-bit elements; how exact they have to be, the bound alone decides.
A program may use at most 256 MiB of HBM per device.

```python
import math
import jax
import jax.numpy as jnp
from jax import lax

S = 256
C = 64
H = 2048
STEPS_DEV = 64
HORIZON = 1024
TRAJ = 32
N_TM = 16


def draw_decay(key, part):
    keys = jax.random.split(key, 6)
    slow_share = 0.5
    slow = jax.random.bernoulli(keys[0], slow_share, (S,))
    slow_rate = jnp.exp(jax.random.uniform(keys[1], (S,), minval=jnp.log(0.1 / HORIZON), maxval=jnp.log(0.5 / HORIZON)))
    fast_rate = jnp.exp(jax.random.uniform(keys[2], (S,), minval=jnp.log(1.0 / 50.0), maxval=jnp.log(1.0 / 30.0)))
    baseline_value = jnp.where(slow, slow_rate, fast_rate)
    multiplier = jnp.exp(jax.random.uniform(keys[3], (HORIZON // STEPS_DEV, S), minval=jnp.log(0.7), maxval=jnp.log(1.4)))
    multiplier = jnp.repeat(multiplier, STEPS_DEV, axis=0)
    spots = jax.random.randint(keys[4], (3,), 0, HORIZON)
    matched_flag = jnp.any(jnp.arange(HORIZON)[:, None] == spots[None, :], axis=1)
    dropped_flag = jax.random.uniform(keys[5], (HORIZON, S), minval=0.5, maxval=0.8)
    sudden_jump = jnp.where(matched_flag[:, None], dropped_flag, 1.0)
    return (jnp.exp(-baseline_value[None, :] * multiplier) * sudden_jump).astype(jnp.float32)


def level_of(rng, shape, shards, low, largest):
    level = 1.0
    for axis_at, blocks in shards:
        heights = jax.random.uniform(jax.random.fold_in(jax.random.fold_in(rng, 6), axis_at), (blocks,), jnp.float32, low / len(shards), largest / len(shards))
        level = level * jnp.repeat(jnp.exp(heights), shape[axis_at] // blocks).reshape((-1,) + (1,) * (len(shape) - 1 - axis_at))
    return level


def noise(key, shape, scale, most, cuts=(), kind=jnp.bfloat16):
    drawn = scale * jax.random.normal(key, shape, jnp.float32)
    if cuts:
        drawn = drawn * level_of(key, shape, cuts, -0.22, 0.18)
    return jnp.clip(drawn, -most, most).astype(kind)


def setup_inputs(seed: int = 0) -> dict:
    splits = jax.random.split(jax.random.key(seed), 10)
    init_state = noise(splits[0], (TRAJ, S), 1.0, 6.0, ((0, 2),), jnp.float32)
    nominal = noise(splits[1], (HORIZON, TRAJ, S), 1.0, 6.0, ((0, 16), (1, 2)))
    target = noise(splits[2], (HORIZON, TRAJ, S), 1.0, 6.0, ((0, 16), (1, 2)))
    decay = draw_decay(jax.random.fold_in(splits[9], 71), 0)
    gain_k = noise(splits[4], (HORIZON, C, S), (S * HORIZON) ** -0.5, 0.01171875, ((0, 16),))
    ctrl_b = noise(splits[5], (S, C), C ** -0.5, 0.75)
    w_in = noise(splits[6], (S, H), S ** -0.5, 0.375)
    hidden_bias = noise(splits[7], (H,), 1.0, 4.0, (), jnp.float32)
    w_out = noise(splits[8], (H, S), H ** -0.5, 0.125)
    return dict(init_state=init_state, nominal=nominal, target=target, decay=decay, gain_k=gain_k, ctrl_b=ctrl_b, w_in=w_in, hidden_bias=hidden_bias, w_out=w_out)


def step_matrix(decay_row, gain_row, ctrl_b):
    coupling = jnp.dot(ctrl_b, gain_row, preferred_element_type=jnp.float32)
    return coupling + jnp.diag(decay_row)

def reference(init_state, nominal, target, decay, gain_k, ctrl_b, w_in, hidden_bias, w_out):
    highest = lax.Precision.HIGHEST
    blocks = nominal.reshape(N_TM, STEPS_DEV * TRAJ, S)

    def network(block):
        pre = jnp.dot(block, w_in, preferred_element_type=jnp.float32) + hidden_bias
        hidden = jax.nn.silu(pre).astype(jnp.bfloat16)
        return jnp.dot(hidden, w_out, preferred_element_type=jnp.float32)
    resid = lax.map(network, blocks).reshape(HORIZON, TRAJ, S)
    spread = jnp.sqrt(1.0 - decay * decay)
    forcing = spread[:, None, :] * resid

    def forward(state, inputs):
        rate, gain, push = inputs
        matrix = step_matrix(rate, gain, ctrl_b)
        state = jnp.dot(state, matrix.T, precision=highest) + push
        return (state, state)
    _, states = lax.scan(forward, init_state, (decay, gain_k, forcing))
    errors = states - target.astype(jnp.float32)

    def backward(carried, inputs):
        rate, gain, miss = inputs
        lam = miss + carried
        matrix = step_matrix(rate, gain, ctrl_b)
        return (jnp.dot(lam, matrix, precision=highest), lam)
    _, lams = lax.scan(backward, jnp.zeros((TRAJ, S), jnp.float32), (decay, gain_k, errors), reverse=True)
    adjoint = (spread[:, None, :] * lams).astype(jnp.bfloat16).reshape(N_TM, STEPS_DEV * TRAJ, S)

    def gradient(carry, inputs):
        block, adj = inputs
        sum_in, sum_out, sum_bias = carry
        pre = jnp.dot(block, w_in, preferred_element_type=jnp.float32) + hidden_bias
        hidden = jax.nn.silu(pre).astype(jnp.bfloat16)
        sum_out = sum_out + jnp.dot(hidden.T, adj, preferred_element_type=jnp.float32)
        dhid = jnp.dot(adj, w_out.T, preferred_element_type=jnp.float32)
        sig = jax.nn.sigmoid(pre)
        dpre = dhid * sig * (1.0 + pre * (1.0 - sig))
        sum_in = sum_in + jnp.dot(block.T, dpre.astype(jnp.bfloat16), preferred_element_type=jnp.float32)
        sum_bias = sum_bias + lax.optimization_barrier(jnp.sum(dpre, axis=0))
        return ((sum_in, sum_out, sum_bias), None)
    start = (jnp.zeros((S, H), jnp.float32), jnp.zeros((H, S), jnp.float32), jnp.zeros((H,), jnp.float32))
    (sum_in, sum_out, sum_bias), _ = lax.scan(gradient, start, (blocks, adjoint))
    scale = 1.0 / math.sqrt(HORIZON * TRAJ)
    return (states, sum_in * scale, sum_out * scale, sum_bias * scale)
```

```python
import functools
import math

import jax
import jax.numpy as jnp
from jax import lax
from jax.experimental import pallas as pl
from jax.experimental.pallas import tpu as pltpu
from jax.sharding import PartitionSpec as P

F32, BF16 = jnp.float32, jnp.bfloat16
CHUNK = 8
GROUP = 4
PIECES = 4
VMEM_LIMIT = 50 * 1024 * 1024


def split(x):
    high = x.astype(BF16)
    return high, (x - high.astype(F32)).astype(BF16)


def dot(a, b):
    return lax.dot_general(a, b, (((1,), (0,)), ((), ())), preferred_element_type=F32)


def dot_t(a, b):
    return lax.dot_general(a, b, (((1,), (1,)), ((), ())), preferred_element_type=F32)


def wide_dot(x, high, low, product=dot):
    rows = x.shape[0]
    x_high, x_low = split(x)
    both = product(jnp.concatenate([x_high, x_low], 0), high)
    return both[:rows] + both[rows:] + product(x_high, low)


def halves(u):
    high, low = split(u)
    lane = lax.broadcasted_iota(jnp.int32, u.shape, 1)
    return jnp.where(lane < u.shape[1] // 2, high.astype(F32), low.astype(F32)).astype(BF16)


def identity(width):
    return (
        lax.broadcasted_iota(jnp.int32, (width, width), 0)
        == lax.broadcasted_iota(jnp.int32, (width, width), 1)
    ).astype(F32)


def maps_kernel(gain, decay, bt2, part, before, after, seg, held):
    chunks, steps, _, width = gain.shape
    for c in range(chunks):
        held[c] = identity(width)

    def step(j, _):
        for c in range(chunks):
            x = held[c]
            high, low = split(x)
            k = gain[c, j]
            k2 = jnp.concatenate([k, k], 0)
            u = dot_t(high, k2) + dot_t(low, k2)
            held[c] = x * decay[c, j] + dot(halves(u), bt2[...])
        return 0

    lax.fori_loop(0, steps, step, 0)
    for c in range(chunks):
        part[0, c], part[1, c] = split(held[c])
    unit = identity(width).astype(BF16)
    zero = jnp.zeros((width, width), BF16)
    before[0, 0], before[1, 0] = unit, zero
    after[0, chunks - 1], after[1, chunks - 1] = unit, zero
    first, last = held[0], held[chunks - 1]
    for c in range(1, chunks):
        before[0, c], before[1, c] = split(first)
        first = wide_dot(first, part[0, c], part[1, c])
        d = chunks - 1 - c
        after[0, d], after[1, d] = split(last)
        if d > 0:
            last = wide_dot(held[d], after[0, d], after[1, d])
    seg[...] = first


def make_maps(gain, decay, bt2):
    chunks, _, _, width = gain.shape
    pair = jax.ShapeDtypeStruct((2, chunks, width, width), BF16)
    vmem = pl.BlockSpec(memory_space=pltpu.VMEM)
    return pl.pallas_call(
        maps_kernel,
        out_shape=(pair, pair, pair, jax.ShapeDtypeStruct((width, width), F32)),
        in_specs=[vmem] * 3,
        out_specs=(vmem,) * 4,
        scratch_shapes=[pltpu.VMEM((chunks, width, width), F32)],
        compiler_params=pltpu.CompilerParams(vmem_limit_bytes=VMEM_LIMIT),
        name="maps",
    )(gain, decay, bt2)


def rollout_kernel(
    count,
    init, forcing, target, decay, spread, gain, bt2, b2, part, before, after, seg,
    states, adjoint,
    segs, prods, vecs, covecs, came, gone, cocame, cogone,
    seg_send, seg_recv, vec_send, vec_recv, covec_send, covec_recv, hop,
):
    chunks, steps, rows, width = forcing.shape
    groups = count // GROUP
    me = lax.axis_index("tm")
    g, slot = me // GROUP, lax.rem(me, GROUP)
    base = g * GROUP

    barrier = pltpu.get_barrier_semaphore()

    def greet(to):
        pl.semaphore_signal(
            barrier, inc=1, device_id={"tm": to}, device_id_type=pl.DeviceIdType.MESH
        )

    for k in range(1, GROUP):
        greet(base + lax.rem(slot + k, GROUP))

    up, down = lax.rem(me + GROUP, count), lax.rem(me - GROUP + count, count)
    greet(up)
    greet(down)
    pl.semaphore_wait(barrier, GROUP + 1)

    def to_group(src, dst, send, recv):
        for k in range(1, GROUP):
            pltpu.make_async_remote_copy(
                src_ref=src, dst_ref=dst.at[slot], send_sem=send.at[k], recv_sem=recv.at[slot],
                device_id={"tm": base + lax.rem(slot + k, GROUP)},
                device_id_type=pl.DeviceIdType.MESH,
            ).start()

    def from_group(src, dst, send, recv):
        for k in range(1, GROUP):
            peer = lax.rem(slot + k, GROUP)
            copy = pltpu.make_async_remote_copy(
                src_ref=src, dst_ref=dst.at[peer], send_sem=send.at[k], recv_sem=recv.at[peer],
                device_id={"tm": base + peer}, device_id_type=pl.DeviceIdType.MESH,
            )
            copy.wait_send()
            copy.wait_recv()

    to_group(seg, segs, seg_send, seg_recv)

    def gain2(c, j):
        k = gain[c, j]
        return jnp.concatenate([k, k], 0)

    def forward(start, emit):
        def step(j, x):
            high, low = split(x)
            outs = []
            for c in range(chunks):
                z = dot_t(jnp.concatenate([high[c], low[c]], 0), gain2(c, j))
                outs.append(z[:rows] + z[rows:])
            push = dot(halves(jnp.concatenate(outs, 0)), bt2[...])
            x = x * decay[:, j] + push.reshape(x.shape) + forcing[:, j]
            if emit:
                states[:, j] = x
            return x

        return lax.fori_loop(0, steps, step, start)

    def backward(start, emit):
        def step(i, nu):
            j = steps - 1 - i
            lam = states[:, j] - target[:, j].astype(F32) + nu
            if emit:
                adjoint[:, j] = (spread[:, j] * lam).astype(BF16)
            high, low = split(lam.reshape(chunks * rows, width))
            z = dot(jnp.concatenate([high, low], 0), b2[...])
            u = halves(z[: chunks * rows] + z[chunks * rows :])
            outs = [
                dot(u[c * rows : (c + 1) * rows], gain2(c, j)).reshape(1, rows, width)
                for c in range(chunks)
            ]
            return lam * decay[:, j] + jnp.concatenate(outs, 0)

        return lax.fori_loop(0, steps, step, start)

    blank = jnp.zeros((chunks, rows, width), F32)
    one = jnp.zeros((rows, width), F32)

    ends = forward(blank, False)
    vec = ends[chunks - 1]
    for c in range(chunks - 1):
        vec = vec + wide_dot(ends[c], after[0, c], after[1, c])
    vecs[slot] = vec
    to_group(vecs.at[slot], vecs, vec_send, vec_recv)

    starts = [one]
    for c in range(chunks - 1):
        x = starts[-1]
        starts.append(ends[c] if c == 0 else wide_dot(x, part[0, c], part[1, c]) + ends[c])

    from_group(seg, segs, seg_send, seg_recv)
    segs[slot] = seg[...]
    unit = identity(width)
    ahead = unit
    for k in range(GROUP):
        ahead = jnp.where(k == slot, prods[0] if k > 0 else unit, ahead)
        if k == 0:
            prods[0] = segs[0]
        else:
            high, low = split(segs[k])
            prods[0] = wide_dot(prods[0], high, low)
    behind = unit
    prods[1] = unit
    for k in range(GROUP - 1, 0, -1):
        high, low = split(prods[1])
        prods[1] = wide_dot(segs[k], high, low)
        behind = jnp.where(k - 1 == slot, prods[1], behind)
    all_high, all_low = split(prods[0])
    ahead_high, ahead_low = split(ahead)
    behind_high, behind_low = split(behind)

    from_group(vecs.at[slot], vecs, vec_send, vec_recv)
    mine, total = one, vecs[0]
    for k in range(1, GROUP):
        mine = jnp.where(k == slot, total, mine)
        high, low = split(segs[k])
        total = wide_dot(total, high, low) + vecs[k]

    def hop_copy(src, dst, which, to):
        return pltpu.make_async_remote_copy(
            src_ref=src, dst_ref=dst, send_sem=hop.at[which, 0], recv_sem=hop.at[which, 1],
            device_id={"tm": to}, device_id_type=pl.DeviceIdType.MESH,
        )

    @pl.when(g == 0)
    def _():
        came[...] = init[...]

    @pl.when(g > 0)
    def _():
        hop_copy(gone, came, 0, up).wait_recv()

    entry = came[...]

    @pl.when(g < groups - 1)
    def _():
        gone[...] = wide_dot(entry, all_high, all_low) + total
        hop_copy(gone, came, 0, up).start()

    begin = wide_dot(entry, ahead_high, ahead_low) + mine
    starts = [
        (begin if c == 0 else wide_dot(begin, before[0, c], before[1, c]) + starts[c]).reshape(
            1, rows, width
        )
        for c in range(chunks)
    ]
    forward(jnp.concatenate(starts, 0), True)

    ends = backward(blank, False)
    vec = ends[0]
    for c in range(1, chunks):
        vec = vec + wide_dot(ends[c], before[0, c], before[1, c], dot_t)
    covecs[slot] = vec
    to_group(covecs.at[slot], covecs, covec_send, covec_recv)
    finals = [one] * chunks
    for c in range(chunks - 2, -1, -1):
        x = finals[c + 1]
        moved = ends[c + 1]
        if c < chunks - 2:
            moved = moved + wide_dot(x, part[0, c + 1], part[1, c + 1], dot_t)
        finals[c] = moved
    from_group(covecs.at[slot], covecs, covec_send, covec_recv)
    mine, total = one, covecs[GROUP - 1]
    for k in range(GROUP - 2, -1, -1):
        mine = jnp.where(k == slot, total, mine)
        high, low = split(segs[k])
        total = wide_dot(total, high, low, dot_t) + covecs[k]

    @pl.when(g == groups - 1)
    def _():
        cocame[...] = jnp.zeros_like(cocame)

    @pl.when(g < groups - 1)
    def _():
        hop_copy(cogone, cocame, 1, down).wait_recv()

    entry = cocame[...]

    @pl.when(g > 0)
    def _():
        cogone[...] = wide_dot(entry, all_high, all_low, dot_t) + total
        hop_copy(cogone, cocame, 1, down).start()

    begin = wide_dot(entry, behind_high, behind_low, dot_t) + mine
    finals = [
        (
            begin
            if c == chunks - 1
            else wide_dot(begin, after[0, c], after[1, c], dot_t) + finals[c]
        ).reshape(1, rows, width)
        for c in range(chunks)
    ]
    backward(jnp.concatenate(finals, 0), True)

    @pl.when(g < groups - 1)
    def _():
        hop_copy(gone, came, 0, up).wait_send()

    @pl.when(g > 0)
    def _():
        hop_copy(cogone, cocame, 1, down).wait_send()


def rollout(count, init, forcing, target, decay, spread, gain, bt2, b2, part, before, after, seg):
    chunks, steps, rows, width = forcing.shape
    vmem = pl.BlockSpec(memory_space=pltpu.VMEM)
    small = pltpu.VMEM((rows, width), F32)
    sems = pltpu.SemaphoreType.DMA((GROUP,))
    return pl.pallas_call(
        functools.partial(rollout_kernel, count),
        out_shape=(
            jax.ShapeDtypeStruct(forcing.shape, F32),
            jax.ShapeDtypeStruct(forcing.shape, BF16),
        ),
        in_specs=[vmem] * 12,
        out_specs=(vmem, vmem),
        scratch_shapes=[
            pltpu.VMEM((GROUP, width, width), F32),
            pltpu.VMEM((2, width, width), F32),
            pltpu.VMEM((GROUP, rows, width), F32),
            pltpu.VMEM((GROUP, rows, width), F32),
            small, small, small, small,
            sems, sems, sems, sems, sems, sems,
            pltpu.SemaphoreType.DMA((2, 2)),
        ],
        compiler_params=pltpu.CompilerParams(
            collective_id=0, has_side_effects=True, vmem_limit_bytes=VMEM_LIMIT
        ),
        name="rollout",
    )(init, forcing, target, decay, spread, gain, bt2, b2, part, before, after, seg)


def reduce_kernel(
    count, pieces,
    first, second, bias, out, bias_out,
    sib, acc, group_in, line_acc, line_in, bias_sib, bias_group, bias_line,
    sib_sems, group_sems, line_sems, spread_sems, share_sems, bias_sib_sems, bias_group_sems,
    bias_line_sems,
):
    groups = count // GROUP
    me, core = lax.axis_index("tm"), lax.axis_index("traj")
    g, slot = me // GROUP, lax.rem(me, GROUP)
    other = 1 - core
    half = first.shape[0] // 2
    piece = 2 * half // pieces
    part = piece // GROUP
    small = part // groups

    def peer(k):
        return lax.rem(slot + k, GROUP)

    def line(k):
        return lax.rem(g + k, groups)

    def at_peer(k):
        return {"tm": g * GROUP + peer(k)}

    def at_line(k):
        return {"tm": line(k) * GROUP + slot}

    barrier = pltpu.get_barrier_semaphore()
    targets = (
        [{"traj": other}]
        + [at_peer(k) for k in range(1, GROUP)]
        + [at_line(k) for k in range(1, groups)]
    )
    for to in targets:
        pl.semaphore_signal(barrier, inc=1, device_id=to, device_id_type=pl.DeviceIdType.MESH)
    pl.semaphore_wait(barrier, len(targets))

    def remote(src, dst, send, recv, to):
        return pltpu.make_async_remote_copy(
            src_ref=src, dst_ref=dst, send_sem=send, recv_sem=recv, device_id=to,
            device_id_type=pl.DeviceIdType.MESH,
        )

    def source(p, which):
        ref = first if p < pieces // 2 else second
        at = (p % (pieces // 2)) * piece
        return ref.at[pl.ds(pl.multiple_of(which * half + at, 8), piece)]

    def sib_copy(p):
        return remote(
            source(p, other), sib.at[p], sib_sems.at[0, p], sib_sems.at[1, p], {"traj": other}
        )

    def bias_sib_copy():
        return remote(
            bias.at[other], bias_sib, bias_sib_sems.at[0], bias_sib_sems.at[1], {"traj": other}
        )

    def group_copy(p, k, there):
        return remote(
            acc.at[p, pl.ds(pl.multiple_of(peer(k) * part, 8), part)], group_in.at[p, there],
            group_sems.at[0, p, k], group_sems.at[1, p, there], at_peer(k),
        )

    def line_copy(p, k, there):
        return remote(
            line_acc.at[p, pl.ds(pl.multiple_of(line(k) * small, 8), small)],
            line_in.at[p, there], line_sems.at[0, p, k], line_sems.at[1, p, there], at_line(k),
        )

    def spread_copy(p, k, there):
        at = pl.multiple_of(p * piece + slot * part + there * small, 8)
        here = pl.multiple_of(p * piece + slot * part + g * small, 8)
        return remote(
            out.at[pl.ds(here, small)], out.at[pl.ds(at, small)],
            spread_sems.at[0, p, k], spread_sems.at[1, p, there], at_line(k),
        )

    def share_copy(p, k, there):
        at = pl.multiple_of(p * piece + there * part, 8)
        here = pl.multiple_of(p * piece + slot * part, 8)
        return remote(
            out.at[pl.ds(here, part)], out.at[pl.ds(at, part)],
            share_sems.at[0, p, k], share_sems.at[1, p, there], at_peer(k),
        )

    def bias_group_copy(k, there):
        return remote(
            bias_group.at[slot], bias_group.at[there], bias_group_sems.at[0, k],
            bias_group_sems.at[1, there], at_peer(k),
        )

    def bias_line_copy(k, there):
        return remote(
            bias_line.at[g], bias_line.at[there], bias_line_sems.at[0, k],
            bias_line_sems.at[1, there], at_line(k),
        )

    for p in range(pieces):
        sib_copy(p).start()
    bias_sib_copy().start()
    for p in range(pieces):
        sib_copy(p).wait_recv()
        acc[p] = source(p, core)[...] + sib[p]
        for k in range(1, GROUP):
            group_copy(p, k, slot).start()
    bias_sib_copy().wait_recv()
    bias_group[slot] = bias[core] + bias_sib[...]
    for k in range(1, GROUP):
        bias_group_copy(k, slot).start()
    for p in range(pieces):
        total = acc[p, pl.ds(pl.multiple_of(slot * part, 8), part)]
        for k in range(1, GROUP):
            group_copy(p, k, peer(k)).wait_recv()
            total = total + group_in[p, peer(k)]
        line_acc[p] = total
        for k in range(1, groups):
            line_copy(p, k, g).start()
    for k in range(1, GROUP):
        bias_group_copy(k, peer(k)).wait_recv()
        bias_group_copy(k, slot).wait_send()
    total = bias_group[0]
    for k in range(1, GROUP):
        total = total + bias_group[k]
    bias_line[g] = total
    for k in range(1, groups):
        bias_line_copy(k, g).start()
    for p in range(pieces):
        total = line_acc[p, pl.ds(pl.multiple_of(g * small, 8), small)]
        for k in range(1, groups):
            line_copy(p, k, line(k)).wait_recv()
            total = total + line_in[p, line(k)]
        out[pl.ds(pl.multiple_of(p * piece + slot * part + g * small, 8), small)] = total
        for k in range(1, groups):
            spread_copy(p, k, g).start()
    for p in range(pieces):
        for k in range(1, groups):
            spread_copy(p, k, line(k)).wait_recv()
        for k in range(1, GROUP):
            share_copy(p, k, slot).start()
    for k in range(1, groups):
        bias_line_copy(k, line(k)).wait_recv()
    total = bias_line[0]
    for k in range(1, groups):
        total = total + bias_line[k]
    bias_out[...] = total
    for p in range(pieces):
        for k in range(1, GROUP):
            share_copy(p, k, peer(k)).wait_recv()
    bias_sib_copy().wait_send()
    for k in range(1, groups):
        bias_line_copy(k, g).wait_send()
    for p in range(pieces):
        sib_copy(p).wait_send()
        for k in range(1, GROUP):
            group_copy(p, k, slot).wait_send()
            share_copy(p, k, slot).wait_send()
        for k in range(1, groups):
            line_copy(p, k, g).wait_send()
            spread_copy(p, k, g).wait_send()


def reduce_all(count, first, second, bias):
    rows, width = first.shape
    groups = count // GROUP
    pieces = max(2, min(PIECES, rows // (GROUP * groups * 8)))
    piece = rows // pieces
    part = piece // GROUP
    small = part // groups
    vmem = pl.BlockSpec(memory_space=pltpu.VMEM)
    dma = pltpu.SemaphoreType.DMA
    tile = bias.shape[1:]
    return pl.pallas_call(
        functools.partial(reduce_kernel, count, pieces),
        out_shape=(
            jax.ShapeDtypeStruct((rows, width), F32),
            jax.ShapeDtypeStruct(tile, F32),
        ),
        in_specs=[vmem] * 3,
        out_specs=(vmem, vmem),
        scratch_shapes=[
            pltpu.VMEM((pieces, piece, width), F32),
            pltpu.VMEM((pieces, piece, width), F32),
            pltpu.VMEM((pieces, GROUP, part, width), F32),
            pltpu.VMEM((pieces, part, width), F32),
            pltpu.VMEM((pieces, groups, small, width), F32),
            pltpu.VMEM(tile, F32),
            pltpu.VMEM((GROUP,) + tile, F32),
            pltpu.VMEM((groups,) + tile, F32),
            dma((2, pieces)),
            dma((2, pieces, GROUP)),
            dma((2, pieces, groups)),
            dma((2, pieces, groups)),
            dma((2, pieces, GROUP)),
            dma((2,)),
            dma((2, GROUP)),
            dma((2, groups)),
        ],
        compiler_params=pltpu.CompilerParams(
            collective_id=1, has_side_effects=True, vmem_limit_bytes=VMEM_LIMIT
        ),
        name="reduce",
    )(first, second, bias)


def shards(init_state, nominal, target, decay, gain_k, ctrl_b, w_in, hidden_bias, w_out):
    steps, rows, width = nominal.shape
    count = lax.axis_size("tm")
    scale = 1.0 / math.sqrt(steps * count * rows * lax.axis_size("traj"))
    chunks = steps // CHUNK
    chunked = (chunks, CHUNK, rows, width)
    gain = gain_k.reshape(chunks, CHUNK, -1, width)
    rates = decay.reshape(chunks, CHUNK, 1, width)
    bt = ctrl_b.T
    bt2 = jnp.concatenate([bt, bt], 0)
    b2 = jnp.concatenate([ctrl_b, ctrl_b], 1)
    part, before, after, seg = make_maps(gain, rates, bt2)

    flat = nominal.reshape(steps * rows, width)
    pre = jnp.dot(flat, w_in, preferred_element_type=F32) + hidden_bias
    hidden = jax.nn.silu(pre).astype(BF16)
    resid = jnp.dot(hidden, w_out, preferred_element_type=F32).reshape(steps, rows, width)
    spread = jnp.sqrt(1.0 - decay * decay)
    forcing = spread[:, None, :] * resid

    states, adjoint = rollout(
        count, init_state, forcing.reshape(chunked), target.reshape(chunked), rates,
        spread.reshape(rates.shape), gain, bt2, b2, part, before, after, seg,
    )
    states = states.reshape(steps, rows, width)
    adjoint = adjoint.reshape(steps * rows, width)

    owg = jnp.einsum("rh,rs->hs", hidden, adjoint, preferred_element_type=F32) * scale
    dhid = jnp.einsum("rs,hs->rh", adjoint, w_out, preferred_element_type=F32)
    sig = jax.nn.sigmoid(pre)
    dpre = dhid * sig * (1.0 + pre * (1.0 - sig))
    grad_in = (
        jnp.einsum("rh,rs->hs", dpre.astype(BF16), flat, preferred_element_type=F32) * scale
    )
    grad_bias = jnp.sum(dpre, axis=0) * scale
    both, grad_bias = reduce_all(count, grad_in, owg, grad_bias.reshape(2, -1, 128))
    half = both.shape[0] // 2
    grad_in, owg, grad_bias = both[:half].T, both[half:], grad_bias.reshape(-1)
    return (states, grad_in, owg, grad_bias)


def solution(mesh):
    in_specs = (
        P("traj", None),
        P("tm", "traj", None),
        P("tm", "traj", None),
        P("tm", None),
        P("tm", None, None),
        P(),
        P(),
        P(),
        P(),
    )
    out_specs = (P("tm", "traj", None), P(None, "traj"), P("traj", None), P("traj"))
    return jax.shard_map(shards, mesh=mesh, in_specs=in_specs, out_specs=out_specs, check_vma=False)
```

```python
import functools
import math

import jax
import jax.numpy as jnp
from jax import lax
from jax.experimental import pallas as pl
from jax.experimental.pallas import tpu as pltpu
from jax.sharding import PartitionSpec as P

F32, BF16 = jnp.float32, jnp.bfloat16
CHUNK = 8
GROUP = 4
PIECES = 8
VMEM_LIMIT = 50 * 1024 * 1024


def split(x):
    high = x.astype(BF16)
    return high, (x - high.astype(F32)).astype(BF16)


def dot(a, b):
    return lax.dot_general(a, b, (((1,), (0,)), ((), ())), preferred_element_type=F32)


def dot_t(a, b):
    return lax.dot_general(a, b, (((1,), (1,)), ((), ())), preferred_element_type=F32)


def wide_dot(x, high, low, product=dot):
    rows = x.shape[0]
    x_high, x_low = split(x)
    both = product(jnp.concatenate([x_high, x_low], 0), high)
    return both[:rows] + both[rows:] + product(x_high, low)


def halves(u):
    high, low = split(u)
    lane = lax.broadcasted_iota(jnp.int32, u.shape, 1)
    return jnp.where(lane < u.shape[1] // 2, high.astype(F32), low.astype(F32)).astype(BF16)


def identity(width):
    return (
        lax.broadcasted_iota(jnp.int32, (width, width), 0)
        == lax.broadcasted_iota(jnp.int32, (width, width), 1)
    ).astype(F32)


def maps_kernel(gain, decay, bt2, part, before, after, seg, held):
    chunks, steps, _, width = gain.shape
    for c in range(chunks):
        held[c] = identity(width)

    def step(j, _):
        for c in range(chunks):
            x = held[c]
            high, low = split(x)
            k = gain[c, j]
            k2 = jnp.concatenate([k, k], 0)
            u = dot_t(high, k2) + dot_t(low, k2)
            held[c] = x * decay[c, j] + dot(halves(u), bt2[...])
        return 0

    lax.fori_loop(0, steps, step, 0)
    for c in range(chunks):
        part[0, c], part[1, c] = split(held[c])
    unit = identity(width).astype(BF16)
    zero = jnp.zeros((width, width), BF16)
    before[0, 0], before[1, 0] = unit, zero
    after[0, chunks - 1], after[1, chunks - 1] = unit, zero
    first, last = held[0], held[chunks - 1]
    for c in range(1, chunks):
        before[0, c], before[1, c] = split(first)
        first = wide_dot(first, part[0, c], part[1, c])
        d = chunks - 1 - c
        after[0, d], after[1, d] = split(last)
        if d > 0:
            last = wide_dot(held[d], after[0, d], after[1, d])
    seg[...] = first


def make_maps(gain, decay, bt2):
    chunks, _, _, width = gain.shape
    pair = jax.ShapeDtypeStruct((2, chunks, width, width), BF16)
    vmem = pl.BlockSpec(memory_space=pltpu.VMEM)
    return pl.pallas_call(
        maps_kernel,
        out_shape=(pair, pair, pair, jax.ShapeDtypeStruct((width, width), F32)),
        in_specs=[vmem] * 3,
        out_specs=(vmem,) * 4,
        scratch_shapes=[pltpu.VMEM((chunks, width, width), F32)],
        compiler_params=pltpu.CompilerParams(vmem_limit_bytes=VMEM_LIMIT),
        name="maps",
    )(gain, decay, bt2)


def rollout_kernel(
    count,
    init, forcing, target, decay, spread, gain, bt2, b2, part, before, after, seg,
    states, adjoint,
    segs, prods, vecs, covecs, came, gone, cocame, cogone,
    seg_send, seg_recv, vec_send, vec_recv, covec_send, covec_recv, hop,
):
    chunks, steps, rows, width = forcing.shape
    groups = count // GROUP
    me = lax.axis_index("tm")
    g, slot = me // GROUP, lax.rem(me, GROUP)
    base = g * GROUP

    barrier = pltpu.get_barrier_semaphore()

    def greet(to):
        pl.semaphore_signal(
            barrier, inc=1, device_id={"tm": to}, device_id_type=pl.DeviceIdType.MESH
        )

    for k in range(1, GROUP):
        greet(base + lax.rem(slot + k, GROUP))

    up, down = lax.rem(me + GROUP, count), lax.rem(me - GROUP + count, count)
    greet(up)
    greet(down)
    pl.semaphore_wait(barrier, GROUP + 1)

    def to_group(src, dst, send, recv):
        for k in range(1, GROUP):
            pltpu.make_async_remote_copy(
                src_ref=src, dst_ref=dst.at[slot], send_sem=send.at[k], recv_sem=recv.at[slot],
                device_id={"tm": base + lax.rem(slot + k, GROUP)},
                device_id_type=pl.DeviceIdType.MESH,
            ).start()

    def from_group(src, dst, send, recv):
        for k in range(1, GROUP):
            peer = lax.rem(slot + k, GROUP)
            copy = pltpu.make_async_remote_copy(
                src_ref=src, dst_ref=dst.at[peer], send_sem=send.at[k], recv_sem=recv.at[peer],
                device_id={"tm": base + peer}, device_id_type=pl.DeviceIdType.MESH,
            )
            copy.wait_send()
            copy.wait_recv()

    to_group(seg, segs, seg_send, seg_recv)

    def gain2(c, j):
        k = gain[c, j]
        return jnp.concatenate([k, k], 0)

    def forward(start, emit):
        def step(j, x):
            high, low = split(x)
            outs = []
            for c in range(chunks):
                z = dot_t(jnp.concatenate([high[c], low[c]], 0), gain2(c, j))
                outs.append(z[:rows] + z[rows:])
            push = dot(halves(jnp.concatenate(outs, 0)), bt2[...])
            x = x * decay[:, j] + push.reshape(x.shape) + forcing[:, j]
            if emit:
                states[:, j] = x
            return x

        return lax.fori_loop(0, steps, step, start)

    def backward(start, emit):
        def step(i, nu):
            j = steps - 1 - i
            lam = states[:, j] - target[:, j].astype(F32) + nu
            if emit:
                adjoint[:, j] = (spread[:, j] * lam).astype(BF16)
            high, low = split(lam.reshape(chunks * rows, width))
            z = dot(jnp.concatenate([high, low], 0), b2[...])
            u = halves(z[: chunks * rows] + z[chunks * rows :])
            outs = [
                dot(u[c * rows : (c + 1) * rows], gain2(c, j)).reshape(1, rows, width)
                for c in range(chunks)
            ]
            return lam * decay[:, j] + jnp.concatenate(outs, 0)

        return lax.fori_loop(0, steps, step, start)

    blank = jnp.zeros((chunks, rows, width), F32)
    one = jnp.zeros((rows, width), F32)

    ends = forward(blank, False)
    vec = ends[chunks - 1]
    for c in range(chunks - 1):
        vec = vec + wide_dot(ends[c], after[0, c], after[1, c])
    vecs[slot] = vec
    to_group(vecs.at[slot], vecs, vec_send, vec_recv)

    starts = [one]
    for c in range(chunks - 1):
        x = starts[-1]
        starts.append(ends[c] if c == 0 else wide_dot(x, part[0, c], part[1, c]) + ends[c])

    from_group(seg, segs, seg_send, seg_recv)
    segs[slot] = seg[...]
    unit = identity(width)
    ahead = unit
    for k in range(GROUP):
        ahead = jnp.where(k == slot, prods[0] if k > 0 else unit, ahead)
        if k == 0:
            prods[0] = segs[0]
        else:
            high, low = split(segs[k])
            prods[0] = wide_dot(prods[0], high, low)
    behind = unit
    prods[1] = unit
    for k in range(GROUP - 1, 0, -1):
        high, low = split(prods[1])
        prods[1] = wide_dot(segs[k], high, low)
        behind = jnp.where(k - 1 == slot, prods[1], behind)
    all_high, all_low = split(prods[0])
    ahead_high, ahead_low = split(ahead)
    behind_high, behind_low = split(behind)

    from_group(vecs.at[slot], vecs, vec_send, vec_recv)
    mine, total = one, vecs[0]
    for k in range(1, GROUP):
        mine = jnp.where(k == slot, total, mine)
        high, low = split(segs[k])
        total = wide_dot(total, high, low) + vecs[k]

    def hop_copy(src, dst, which, to):
        return pltpu.make_async_remote_copy(
            src_ref=src, dst_ref=dst, send_sem=hop.at[which, 0], recv_sem=hop.at[which, 1],
            device_id={"tm": to}, device_id_type=pl.DeviceIdType.MESH,
        )

    @pl.when(g == 0)
    def _():
        came[...] = init[...]

    @pl.when(g > 0)
    def _():
        hop_copy(gone, came, 0, up).wait_recv()

    entry = came[...]

    @pl.when(g < groups - 1)
    def _():
        gone[...] = wide_dot(entry, all_high, all_low) + total
        hop_copy(gone, came, 0, up).start()

    begin = wide_dot(entry, ahead_high, ahead_low) + mine
    starts = [
        (begin if c == 0 else wide_dot(begin, before[0, c], before[1, c]) + starts[c]).reshape(
            1, rows, width
        )
        for c in range(chunks)
    ]
    forward(jnp.concatenate(starts, 0), True)

    ends = backward(blank, False)
    vec = ends[0]
    for c in range(1, chunks):
        vec = vec + wide_dot(ends[c], before[0, c], before[1, c], dot_t)
    covecs[slot] = vec
    to_group(covecs.at[slot], covecs, covec_send, covec_recv)
    finals = [one] * chunks
    for c in range(chunks - 2, -1, -1):
        x = finals[c + 1]
        moved = ends[c + 1]
        if c < chunks - 2:
            moved = moved + wide_dot(x, part[0, c + 1], part[1, c + 1], dot_t)
        finals[c] = moved
    from_group(covecs.at[slot], covecs, covec_send, covec_recv)
    mine, total = one, covecs[GROUP - 1]
    for k in range(GROUP - 2, -1, -1):
        mine = jnp.where(k == slot, total, mine)
        high, low = split(segs[k])
        total = wide_dot(total, high, low, dot_t) + covecs[k]

    @pl.when(g == groups - 1)
    def _():
        cocame[...] = jnp.zeros_like(cocame)

    @pl.when(g < groups - 1)
    def _():
        hop_copy(cogone, cocame, 1, down).wait_recv()

    entry = cocame[...]

    @pl.when(g > 0)
    def _():
        cogone[...] = wide_dot(entry, all_high, all_low, dot_t) + total
        hop_copy(cogone, cocame, 1, down).start()

    begin = wide_dot(entry, behind_high, behind_low, dot_t) + mine
    finals = [
        (
            begin
            if c == chunks - 1
            else wide_dot(begin, after[0, c], after[1, c], dot_t) + finals[c]
        ).reshape(1, rows, width)
        for c in range(chunks)
    ]
    backward(jnp.concatenate(finals, 0), True)

    @pl.when(g < groups - 1)
    def _():
        hop_copy(gone, came, 0, up).wait_send()

    @pl.when(g > 0)
    def _():
        hop_copy(cogone, cocame, 1, down).wait_send()


def rollout(count, init, forcing, target, decay, spread, gain, bt2, b2, part, before, after, seg):
    chunks, steps, rows, width = forcing.shape
    vmem = pl.BlockSpec(memory_space=pltpu.VMEM)
    small = pltpu.VMEM((rows, width), F32)
    sems = pltpu.SemaphoreType.DMA((GROUP,))
    return pl.pallas_call(
        functools.partial(rollout_kernel, count),
        out_shape=(
            jax.ShapeDtypeStruct(forcing.shape, F32),
            jax.ShapeDtypeStruct(forcing.shape, BF16),
        ),
        in_specs=[vmem] * 12,
        out_specs=(vmem, vmem),
        scratch_shapes=[
            pltpu.VMEM((GROUP, width, width), F32),
            pltpu.VMEM((2, width, width), F32),
            pltpu.VMEM((GROUP, rows, width), F32),
            pltpu.VMEM((GROUP, rows, width), F32),
            small, small, small, small,
            sems, sems, sems, sems, sems, sems,
            pltpu.SemaphoreType.DMA((2, 2)),
        ],
        compiler_params=pltpu.CompilerParams(
            collective_id=0, has_side_effects=True, vmem_limit_bytes=VMEM_LIMIT
        ),
        name="rollout",
    )(init, forcing, target, decay, spread, gain, bt2, b2, part, before, after, seg)


def reduce_kernel(
    count, pieces,
    first, second, bias, out, bias_out,
    sib, acc, group_in, line_acc, line_in, bias_sib, bias_group, bias_line,
    sib_sems, group_sems, line_sems, spread_sems, share_sems, bias_sib_sems, bias_group_sems,
    bias_line_sems,
):
    groups = count // GROUP
    me, core = lax.axis_index("tm"), lax.axis_index("traj")
    g, slot = me // GROUP, lax.rem(me, GROUP)
    other = 1 - core
    half = first.shape[0] // 2
    piece = 2 * half // pieces
    part = piece // GROUP
    small = part // groups

    def peer(k):
        return lax.rem(slot + k, GROUP)

    def line(k):
        return lax.rem(g + k, groups)

    def at_peer(k):
        return {"tm": g * GROUP + peer(k)}

    def at_line(k):
        return {"tm": line(k) * GROUP + slot}

    barrier = pltpu.get_barrier_semaphore()
    targets = (
        [{"traj": other}]
        + [at_peer(k) for k in range(1, GROUP)]
        + [at_line(k) for k in range(1, groups)]
    )
    for to in targets:
        pl.semaphore_signal(barrier, inc=1, device_id=to, device_id_type=pl.DeviceIdType.MESH)
    pl.semaphore_wait(barrier, len(targets))

    def remote(src, dst, send, recv, to):
        return pltpu.make_async_remote_copy(
            src_ref=src, dst_ref=dst, send_sem=send, recv_sem=recv, device_id=to,
            device_id_type=pl.DeviceIdType.MESH,
        )

    def source(p, which):
        ref = first if p < pieces // 2 else second
        at = (p % (pieces // 2)) * piece
        return ref.at[pl.ds(pl.multiple_of(which * half + at, 8), piece)]

    def sib_copy(p):
        return remote(
            source(p, other), sib.at[p], sib_sems.at[0, p], sib_sems.at[1, p], {"traj": other}
        )

    def bias_sib_copy():
        return remote(
            bias.at[other], bias_sib, bias_sib_sems.at[0], bias_sib_sems.at[1], {"traj": other}
        )

    def group_copy(p, k, there):
        return remote(
            acc.at[p, pl.ds(pl.multiple_of(peer(k) * part, 8), part)], group_in.at[p, there],
            group_sems.at[0, p, k], group_sems.at[1, p, there], at_peer(k),
        )

    def line_copy(p, k, there):
        return remote(
            line_acc.at[p, pl.ds(pl.multiple_of(line(k) * small, 8), small)],
            line_in.at[p, there], line_sems.at[0, p, k], line_sems.at[1, p, there], at_line(k),
        )

    def spread_copy(p, k, there):
        at = pl.multiple_of(p * piece + slot * part + there * small, 8)
        here = pl.multiple_of(p * piece + slot * part + g * small, 8)
        return remote(
            out.at[pl.ds(here, small)], out.at[pl.ds(at, small)],
            spread_sems.at[0, p, k], spread_sems.at[1, p, there], at_line(k),
        )

    def share_copy(p, k, there):
        at = pl.multiple_of(p * piece + there * part, 8)
        here = pl.multiple_of(p * piece + slot * part, 8)
        return remote(
            out.at[pl.ds(here, part)], out.at[pl.ds(at, part)],
            share_sems.at[0, p, k], share_sems.at[1, p, there], at_peer(k),
        )

    def bias_group_copy(k, there):
        return remote(
            bias_group.at[slot], bias_group.at[there], bias_group_sems.at[0, k],
            bias_group_sems.at[1, there], at_peer(k),
        )

    def bias_line_copy(k, there):
        return remote(
            bias_line.at[g], bias_line.at[there], bias_line_sems.at[0, k],
            bias_line_sems.at[1, there], at_line(k),
        )

    for p in range(pieces):
        sib_copy(p).start()
    bias_sib_copy().start()
    for p in range(pieces):
        sib_copy(p).wait_recv()
        acc[p] = source(p, core)[...] + sib[p]
        for k in range(1, GROUP):
            group_copy(p, k, slot).start()
    bias_sib_copy().wait_recv()
    bias_group[slot] = bias[core] + bias_sib[...]
    for k in range(1, GROUP):
        bias_group_copy(k, slot).start()
    for p in range(pieces):
        total = acc[p, pl.ds(pl.multiple_of(slot * part, 8), part)]
        for k in range(1, GROUP):
            group_copy(p, k, peer(k)).wait_recv()
            total = total + group_in[p, peer(k)]
        line_acc[p] = total
        for k in range(1, groups):
            line_copy(p, k, g).start()
    for k in range(1, GROUP):
        bias_group_copy(k, peer(k)).wait_recv()
        bias_group_copy(k, slot).wait_send()
    total = bias_group[0]
    for k in range(1, GROUP):
        total = total + bias_group[k]
    bias_line[g] = total
    for k in range(1, groups):
        bias_line_copy(k, g).start()
    for p in range(pieces):
        total = line_acc[p, pl.ds(pl.multiple_of(g * small, 8), small)]
        for k in range(1, groups):
            line_copy(p, k, line(k)).wait_recv()
            total = total + line_in[p, line(k)]
        out[pl.ds(pl.multiple_of(p * piece + slot * part + g * small, 8), small)] = total
        for k in range(1, groups):
            spread_copy(p, k, g).start()
    for p in range(pieces):
        for k in range(1, groups):
            spread_copy(p, k, line(k)).wait_recv()
        for k in range(1, GROUP):
            share_copy(p, k, slot).start()
    for k in range(1, groups):
        bias_line_copy(k, line(k)).wait_recv()
    total = bias_line[0]
    for k in range(1, groups):
        total = total + bias_line[k]
    bias_out[...] = total
    for p in range(pieces):
        for k in range(1, GROUP):
            share_copy(p, k, peer(k)).wait_recv()
    bias_sib_copy().wait_send()
    for k in range(1, groups):
        bias_line_copy(k, g).wait_send()
    for p in range(pieces):
        sib_copy(p).wait_send()
        for k in range(1, GROUP):
            group_copy(p, k, slot).wait_send()
            share_copy(p, k, slot).wait_send()
        for k in range(1, groups):
            line_copy(p, k, g).wait_send()
            spread_copy(p, k, g).wait_send()


def reduce_all(count, first, second, bias):
    rows, width = first.shape
    groups = count // GROUP
    pieces = max(2, min(PIECES, rows // (GROUP * groups * 8)))
    piece = rows // pieces
    part = piece // GROUP
    small = part // groups
    vmem = pl.BlockSpec(memory_space=pltpu.VMEM)
    dma = pltpu.SemaphoreType.DMA
    tile = bias.shape[1:]
    return pl.pallas_call(
        functools.partial(reduce_kernel, count, pieces),
        out_shape=(
            jax.ShapeDtypeStruct((rows, width), F32),
            jax.ShapeDtypeStruct(tile, F32),
        ),
        in_specs=[vmem] * 3,
        out_specs=(vmem, vmem),
        scratch_shapes=[
            pltpu.VMEM((pieces, piece, width), F32),
            pltpu.VMEM((pieces, piece, width), F32),
            pltpu.VMEM((pieces, GROUP, part, width), F32),
            pltpu.VMEM((pieces, part, width), F32),
            pltpu.VMEM((pieces, groups, small, width), F32),
            pltpu.VMEM(tile, F32),
            pltpu.VMEM((GROUP,) + tile, F32),
            pltpu.VMEM((groups,) + tile, F32),
            dma((2, pieces)),
            dma((2, pieces, GROUP)),
            dma((2, pieces, groups)),
            dma((2, pieces, groups)),
            dma((2, pieces, GROUP)),
            dma((2,)),
            dma((2, GROUP)),
            dma((2, groups)),
        ],
        compiler_params=pltpu.CompilerParams(
            collective_id=1, has_side_effects=True, vmem_limit_bytes=VMEM_LIMIT
        ),
        name="reduce",
    )(first, second, bias)


def shards(init_state, nominal, target, decay, gain_k, ctrl_b, w_in, hidden_bias, w_out):
    steps, rows, width = nominal.shape
    count = lax.axis_size("tm")
    scale = 1.0 / math.sqrt(steps * count * rows * lax.axis_size("traj"))
    chunks = steps // CHUNK
    chunked = (chunks, CHUNK, rows, width)
    gain = gain_k.reshape(chunks, CHUNK, -1, width)
    rates = decay.reshape(chunks, CHUNK, 1, width)
    bt = ctrl_b.T
    bt2 = jnp.concatenate([bt, bt], 0)
    b2 = jnp.concatenate([ctrl_b, ctrl_b], 1)
    part, before, after, seg = make_maps(gain, rates, bt2)

    flat = nominal.reshape(steps * rows, width)
    pre = jnp.dot(flat, w_in, preferred_element_type=F32) + hidden_bias
    hidden = jax.nn.silu(pre).astype(BF16)
    resid = jnp.dot(hidden, w_out, preferred_element_type=F32).reshape(steps, rows, width)
    spread = jnp.sqrt(1.0 - decay * decay)
    forcing = spread[:, None, :] * resid

    states, adjoint = rollout(
        count, init_state, forcing.reshape(chunked), target.reshape(chunked), rates,
        spread.reshape(rates.shape), gain, bt2, b2, part, before, after, seg,
    )
    states = states.reshape(steps, rows, width)
    adjoint = adjoint.reshape(steps * rows, width)

    owg = jnp.einsum("rh,rs->hs", hidden, adjoint, preferred_element_type=F32) * scale
    dhid = jnp.einsum("rs,hs->rh", adjoint, w_out, preferred_element_type=F32)
    sig = jax.nn.sigmoid(pre)
    dpre = dhid * sig * (1.0 + pre * (1.0 - sig))
    grad_in = (
        jnp.einsum("rh,rs->hs", dpre.astype(BF16), flat, preferred_element_type=F32) * scale
    )
    grad_bias = jnp.sum(dpre, axis=0) * scale
    both, grad_bias = reduce_all(count, grad_in, owg, grad_bias.reshape(2, -1, 128))
    half = both.shape[0] // 2
    grad_in, owg, grad_bias = both[:half].T, both[half:], grad_bias.reshape(-1)
    return (states, grad_in, owg, grad_bias)


def solution(mesh):
    in_specs = (
        P("traj", None),
        P("tm", "traj", None),
        P("tm", "traj", None),
        P("tm", None),
        P("tm", None, None),
        P(),
        P(),
        P(),
        P(),
    )
    out_specs = (P("tm", "traj", None), P(None, "traj"), P("traj", None), P("traj"))
    return jax.shard_map(shards, mesh=mesh, in_specs=in_specs, out_specs=out_specs, check_vma=False)
```
